32 devices in a mesh: groups: 2 (over x), seq: 2 (over core), tensor: 8 (over z, y).
Axes of the slice: x: 2, y: 2, z: 4, core: 2. Of those that a mesh axis runs over, the one named last changes fastest.
Arguments:
- queries: bfloat16 [1536, 16384], P(('groups', 'seq'), 'tensor'), parts along dimension 0, may hold values from -400 to 400
- keys: bfloat16 [1536, 1024], P(('groups', 'seq')), parts along dimension 0, may hold values from -4 to 4
- values: bfloat16 [1536, 1024], P(('groups', 'seq')), parts along dimension 0, may hold values from -24 to 24
- residual: bfloat16 [1536, 16384], P(('groups', 'seq'), 'tensor'), parts along dimension 0, may hold values from -112 to 112
- out_weight: bfloat16 [16384, 16384], P('tensor'), may hold values from -0.125 to 0.125
- norm_gain: bfloat16 [16384], P('tensor'), may hold values from 0.099609375 to 1.8984375
- kv_weight: bfloat16 [16384, 2048], P(None, 'tensor'), may hold values from -0.046875 to 0.046875
Outputs:
- stream: bfloat16 [1536, 16384], P(('groups', 'seq'), 'tensor'), parts along dimension 0
- kv_next: bfloat16 [1536, 2048], P(('groups', 'seq'), 'tensor'), parts along dimension 0
The draws below stay inside these ranges and needn't reach their ends.
There are 2 independent parts, one for each index of `groups`. The reference program is written for one: setup_inputs(seed, part) draws one part's arguments, and reference() takes and returns one part's arrays. A program takes and returns all parts, laid end to end along the dimension named above; an argument that names none is the same for every part. Nothing has to cross between parts.
All inputs are finite; a program needn't handle non-finite values. Where the reference program divides by a largest or mean magnitude, that divisor is 1e-20 or more.
Results may differ from the reference program's by a relative error of at most 0.012.
Values may be sent and summed in bfloat16 or wider, within the bound.
No kernel may reach another device: no remote copies, remote signals or barrier semaphores. Data moves between devices by JAX's collectives and lax.ppermute only.
A program may use at most 320 MiB of HBM per device.

```python
import math
import jax
import jax.numpy as jnp
from jax import lax

D = 16384
Q_HEADS = 128
KV_HEADS = 8
HEAD = 128
BLOCK = 128
TOKENS = 768
N_TENSOR = 8


def key_base(key):
    return jax.random.truncated_normal(key, -4.0, 4.0, (TOKENS, KV_HEADS, HEAD), jnp.float32)


def draw_keys(key, part):
    base = key_base(key)
    return base.reshape(TOKENS, KV_HEADS * HEAD).astype(jnp.bfloat16)


def draw_queries(key, part):
    key = jax.random.fold_in(key, 7)
    first_key = jax.random.fold_in(key, 0)
    base = jax.random.truncated_normal(first_key, -4.0, 4.0, (TOKENS, Q_HEADS, HEAD), jnp.float32)
    return base.reshape(TOKENS, Q_HEADS * HEAD).astype(jnp.bfloat16)


def rising_scale(col_key, rise):
    positions = jnp.arange(D, dtype=jnp.float32)[None, :] / D
    return 0.5 * jnp.exp(positions * math.log(rise)) * jnp.exp(jax.random.uniform(col_key, (1, D), jnp.float32, math.log(0.6), math.log(1.0)))


def draw_residual(key, part):
    key = jax.random.fold_in(key, 11)
    noise_key, row_key, col_key = jax.random.split(key, 3)
    col_scale = rising_scale(col_key, 30.0)
    row_scale = jnp.exp(jax.random.uniform(row_key, (TOKENS, 1), jnp.float32, math.log(0.5), math.log(1.0)))
    noise = jax.random.truncated_normal(noise_key, -4.0, 4.0, (TOKENS, D), jnp.float32)
    return (noise * row_scale * col_scale).astype(jnp.bfloat16)


def with_spikes(array, stream_key, source, target, shards_of, factor):
    def block_of(axis_at):
        return (jnp.arange(array.shape[axis_at]) // (array.shape[axis_at] // shards_of)).reshape((-1,) + (1,) * (array.ndim - 1 - axis_at))

    one_side = jax.random.permutation(stream_key, shards_of)[block_of(target)]
    other_side = (block_of(target) + shards_of // 2) % shards_of
    return jnp.where((block_of(source) == one_side) | (block_of(source) == other_side), factor * array, array)


def block_scale(own_key, shape, shards, least, high):
    loudness, own = 1.0, jax.random.fold_in(own_key, 6)
    for dim, parts in shards:
        draws = jnp.exp(jax.random.uniform(jax.random.fold_in(own, dim), (parts,), jnp.float32, least / len(shards), high / len(shards)))
        loudness = loudness * jnp.repeat(draws, shape[dim] // parts).reshape([-1 if axis == dim else 1 for axis in range(len(shape))])
    return loudness


def gaussian(key, dims, spread, most, cuts=(), kind=jnp.bfloat16):
    gain = block_scale(key, dims, cuts, -0.22, 0.18) if cuts else 1.0
    entries = jax.random.normal(key, dims, jnp.float32) * spread * gain
    return jnp.minimum(jnp.maximum(entries, -most), most).astype(kind)


def noise_with(own_key, shape, spread, bound, cuts, heavy, kind=jnp.bfloat16):
    entries = spread * jax.random.normal(own_key, shape, jnp.float32)
    if cuts:
        entries = entries * block_scale(own_key, shape, cuts, -0.22, 0.18)
    return jnp.clip(with_spikes(entries, jax.random.fold_in(own_key, 3), *heavy), -bound, bound).astype(kind)


def setup_inputs(seed: int = 0, part: int = 0) -> dict:
    key_list = jax.random.split(jax.random.key(seed), 8)
    part_splits = jax.random.split(jax.random.fold_in(key_list[7], part), 8)
    queries = draw_queries(jax.random.fold_in(jax.random.fold_in(key_list[7], part), 71), part)
    keys = draw_keys(jax.random.fold_in(jax.random.fold_in(key_list[7], part), 71), part)
    values = gaussian(part_splits[2], (TOKENS, KV_HEADS * HEAD), 4.0, 24.0, ((0, 2),))
    residual = draw_residual(jax.random.fold_in(jax.random.fold_in(key_list[7], part), 71), part)
    out_weight = noise_with(key_list[4], (Q_HEADS * HEAD, D), (Q_HEADS * HEAD // 4) ** -0.5, 0.125, ((0, 8),), (0, 1, 8, 2.0))
    norm_gain = jnp.clip(1.0 + 0.18 * jax.random.normal(key_list[5], (D,), jnp.float32), 0.099609375, 1.8984375).astype(jnp.bfloat16)
    kv_weight = gaussian(key_list[6], (D, 2 * KV_HEADS * HEAD), D ** -0.5, 0.046875, ((1, 8),))
    return dict(queries=queries, keys=keys, values=values, residual=residual, out_weight=out_weight, norm_gain=norm_gain, kv_weight=kv_weight)


def block_pack(matrix, block_size):
    row_count = matrix.shape[0]
    blocks = matrix.reshape(row_count, matrix.shape[1] // block_size, block_size)
    scales = lax.optimization_barrier(jnp.max(jnp.abs(blocks), axis=2)) + 1e-06
    packed = (blocks / scales[:, :, None]).astype(jnp.bfloat16)
    return (packed, scales)

def attend_group(inputs):
    group_queries, group_keys, group_values = inputs
    row_count = group_queries.shape[0]
    positions = jnp.arange(row_count)
    visible = positions[None, :] <= positions[:, None]
    scores = jnp.einsum('tgd,kd->gtk', group_queries, group_keys) * HEAD ** (-0.5)
    scores = jnp.where(visible[None], scores, -1e+30)
    row_peak = lax.optimization_barrier(jnp.max(scores, axis=2, keepdims=True))
    weights = jnp.exp(scores - row_peak)
    shares = (weights / lax.optimization_barrier(jnp.sum(weights, axis=2, keepdims=True))).astype(jnp.bfloat16)
    context = jnp.einsum('gtk,kd->tgd', shares.astype(jnp.float32), group_values)
    return context.astype(jnp.bfloat16)

def reference(queries, keys, values, residual, out_weight, norm_gain, kv_weight):
    row_count = queries.shape[0]
    group_heads = Q_HEADS // KV_HEADS
    query_groups = queries.astype(jnp.float32).reshape(row_count, KV_HEADS, group_heads, HEAD).transpose(1, 0, 2, 3)
    key_groups = keys.astype(jnp.float32).reshape(row_count, KV_HEADS, HEAD).transpose(1, 0, 2)
    value_groups = values.astype(jnp.float32).reshape(row_count, KV_HEADS, HEAD).transpose(1, 0, 2)
    context = lax.map(attend_group, (query_groups, key_groups, value_groups))
    context = context.transpose(1, 0, 2, 3).reshape(row_count, Q_HEADS * HEAD)
    slab_rows = Q_HEADS * HEAD // N_TENSOR
    context_slabs = context.reshape(row_count, N_TENSOR, slab_rows).transpose(1, 0, 2)
    weight_slabs = out_weight.reshape(N_TENSOR, slab_rows, D)

    def add_device(running, slab):
        partial_out = jnp.dot(slab[0], slab[1], preferred_element_type=jnp.float32)
        packed, scales = block_pack(partial_out, BLOCK)
        rescaled = (packed.astype(jnp.float32) * scales[:, :, None]).reshape(row_count, D)
        return (running + rescaled, None)
    attended = lax.scan(add_device, jnp.zeros((row_count, D), jnp.float32), (context_slabs, weight_slabs))[0]
    stream = (residual.astype(jnp.float32) + attended).astype(jnp.bfloat16)
    widened = stream.astype(jnp.float32)
    inverse = lax.rsqrt(lax.optimization_barrier(jnp.mean(widened * widened, axis=1)) + 1e-05)
    normed = widened * inverse[:, None] * norm_gain.astype(jnp.float32)[None, :]
    norm_packed, norm_scales = block_pack(normed, BLOCK)
    columns = kv_weight.shape[1]
    weight_blocks = kv_weight.reshape(D // BLOCK, BLOCK, columns)

    def add_block(running, item):
        block_packed, block_scales, block_weight = item
        product = jnp.dot(block_packed, block_weight, preferred_element_type=jnp.float32)
        return (running + product * block_scales[:, None], None)
    projected = lax.scan(add_block, jnp.zeros((row_count, columns), jnp.float32), (norm_packed.transpose(1, 0, 2), norm_scales.transpose(1, 0), weight_blocks))[0]
    return (stream, projected.astype(jnp.bfloat16))
```

```python
import functools
import math

import jax
import jax.numpy as jnp
from jax import lax
from jax.experimental import pallas as pl
from jax.experimental.pallas import tpu as pltpu
from jax.sharding import PartitionSpec as P

D = 16384
Q_HEADS = 128
KV_HEADS = 8
HEAD = 128
ROW_CHUNKS = 2
F32 = jnp.float32
BF16 = jnp.bfloat16
LOGIT = HEAD ** (-0.5) * math.log2(math.e)


def attend_kernel(first, seq_ref, q_ref, ek_ref, ev_ref, k_ref, v_ref, out_ref):
    rows = q_ref.shape[0]
    contract = (((1,), (1,)), ((), ()))
    q = q_ref[...]
    early = lax.dot_general(q, ek_ref[...], contract, preferred_element_type=F32)
    early = jnp.where(seq_ref[0] > 0, early, -1e30)
    own = lax.dot_general(q, k_ref[...], contract, preferred_element_type=F32)
    key_pos = lax.broadcasted_iota(jnp.int32, own.shape, 1)
    row_pos = lax.broadcasted_iota(jnp.int32, own.shape, 0) + first
    own = jnp.where(key_pos <= row_pos, own, -1e30)
    peak = jnp.maximum(
        jnp.max(early, axis=1, keepdims=True), jnp.max(own, axis=1, keepdims=True)
    )
    early = jnp.exp2((early - peak) * LOGIT)
    own = jnp.exp2((own - peak) * LOGIT)
    total = jnp.sum(early, axis=1, keepdims=True) + jnp.sum(own, axis=1, keepdims=True)
    context = jnp.dot(early.astype(BF16), ev_ref[...], preferred_element_type=F32)
    context += jnp.dot(own.astype(BF16), v_ref[...], preferred_element_type=F32)
    out_ref[...] = (context / total).astype(BF16)


def attend(queries, early_keys, early_values, own_keys, own_values, seq_index, chunk, rows):
    heads = queries.shape[1] // HEAD
    early = early_keys.shape[0]
    seen = (chunk + 1) * rows
    flops = 4 * heads * rows * (early + seen) * HEAD
    return pl.pallas_call(
        functools.partial(attend_kernel, chunk * rows),
        grid_spec=pltpu.PrefetchScalarGridSpec(
            num_scalar_prefetch=1,
            grid=(heads,),
            in_specs=[
                pl.BlockSpec((rows, HEAD), lambda h, s: (chunk, h)),
                pl.BlockSpec((early, HEAD), lambda h, s: (0, 0)),
                pl.BlockSpec((early, HEAD), lambda h, s: (0, 0)),
                pl.BlockSpec((seen, HEAD), lambda h, s: (0, 0)),
                pl.BlockSpec((seen, HEAD), lambda h, s: (0, 0)),
            ],
            out_specs=pl.BlockSpec((rows, HEAD), lambda h, s: (0, h)),
        ),
        out_shape=jax.ShapeDtypeStruct((rows, heads * HEAD), BF16),
        compiler_params=pltpu.CompilerParams(vmem_limit_bytes=32 * 2**20),
        cost_estimate=pl.CostEstimate(
            flops=flops,
            bytes_accessed=4 * rows * heads * HEAD,
            transcendentals=heads * rows * (early + seen),
        ),
    )(seq_index, queries, early_keys, early_values, own_keys, own_values)


class Chain:
    def __init__(self):
        t = lax.axis_index("tensor")
        self.z, self.y = t // 2, t % 2
        low = self.z < 2
        far = jnp.where(low, 3, 0)
        near = jnp.where(low, 2, 1)
        self.order = (far, near, 6 - far - near - self.z, self.z)

    @staticmethod
    def over(block, pairs):
        return lax.ppermute(block, "tensor", pairs)

    def to_y(self, block):
        return self.over(block, [(i, i ^ 1) for i in range(8)])

    def to_middle(self, block):
        return self.over(block, [(0, 2), (1, 3), (6, 4), (7, 5)])

    def across(self, block):
        return self.over(block, [(2, 4), (3, 5), (4, 2), (5, 3)])

    def to_z1(self, block):
        return self.over(block, [(i, i ^ 2) for i in range(8)])

    def reduce_scatter(self, term):
        got = [
            self.to_y(term(2 * place + 1 - self.y).astype(BF16)) for place in self.order
        ]
        own = [
            term(2 * place + self.y) + got[j].astype(F32)
            for j, place in enumerate(self.order)
        ]
        far = self.to_middle(own[0].astype(BF16))
        near = self.to_middle(own[1].astype(BF16))
        far = self.across((own[0] + far.astype(F32)).astype(BF16))
        near = self.across((own[1] + near.astype(F32)).astype(BF16))
        last = self.to_z1((own[2] + far.astype(F32)).astype(BF16))
        return own[3] + near.astype(F32) + last.astype(F32)

    def total(self, block):
        for step in (1, 2, 4):
            block = block + self.over(block, [(i, i ^ step) for i in range(8)])
        return block

    def relay_weight(self, weight):
        depth, columns = weight.shape
        slab = depth // 8
        part = slab // 4
        group, seq = lax.axis_index("groups"), lax.axis_index("seq")
        quarter = group * 2 + seq
        blocks = weight.reshape(4, 2, 4, part, columns)
        blocks = lax.dynamic_index_in_dim(blocks, quarter, 2, keepdims=False)
        kept = lax.dynamic_index_in_dim(blocks, self.y, 1, keepdims=False)
        sent = lax.dynamic_index_in_dim(blocks, 1 - self.y, 1, keepdims=False)
        got = self.to_y(sent)
        first = self.y == 0
        pair = jnp.stack([jnp.where(first, kept, got), jnp.where(first, got, kept)], axis=1)
        mine = jnp.zeros((4, 2, part, columns), weight.dtype)
        for step in range(4):
            place = self.z ^ step
            piece = lax.dynamic_index_in_dim(pair, place, 0, keepdims=True)
            if step:
                piece = self.over(piece, [(i, i ^ (2 * step)) for i in range(8)])
            mine = lax.dynamic_update_slice_in_dim(mine, piece, place, 0)
        mine = mine.reshape(8, part, columns)
        swap = [(0, 1), (1, 0)]
        other = lax.ppermute(mine, "groups", swap)
        whole = jnp.zeros((8, slab, columns), weight.dtype)
        beside = lax.ppermute((mine, other), "seq", swap)
        for block, g, s in (
            (mine, group, seq),
            (other, 1 - group, seq),
            (beside[0], group, 1 - seq),
            (beside[1], 1 - group, 1 - seq),
        ):
            whole = lax.dynamic_update_slice_in_dim(whole, block, (g * 2 + s) * part, 1)
        return whole


def on_device(queries, keys, values, residual, out_weight, norm_gain, kv_weight):
    tokens = queries.shape[0]
    heads_here = queries.shape[1] // HEAD
    devices = lax.axis_size("tensor")
    width = D // devices
    columns = kv_weight.shape[1]
    tensor_rank = lax.axis_index("tensor")
    seq_index = lax.axis_index("seq")
    kv_group = tensor_rank * heads_here // (Q_HEADS // KV_HEADS)
    own_keys = lax.dynamic_slice_in_dim(keys, kv_group * HEAD, HEAD, 1)
    own_values = lax.dynamic_slice_in_dim(values, kv_group * HEAD, HEAD, 1)
    early_keys, early_values = lax.ppermute((own_keys, own_values), "seq", [(0, 1)])
    gain = norm_gain.astype(F32)[None, :]
    chained = devices == 8
    chunks = ROW_CHUNKS if chained else 1
    rows = tokens // chunks
    if chained:
        chain = Chain()
        slab_weight = chain.relay_weight(kv_weight)
    streams, projections = [], []
    for chunk in range(chunks):
        context = attend(
            queries, early_keys, early_values, own_keys, own_values,
            seq_index.reshape(1), chunk, rows,
        )

        def out_term(t):
            weight = lax.dynamic_slice_in_dim(out_weight, t * width, width, 1)
            return jnp.dot(context, weight, preferred_element_type=F32)

        if chained:
            attended = chain.reduce_scatter(out_term)
        else:
            partial = jnp.dot(context, out_weight, preferred_element_type=F32).astype(BF16)
            attended = lax.psum_scatter(
                partial, "tensor", scatter_dimension=1, tiled=True
            ).astype(F32)
        start = residual[chunk * rows : (chunk + 1) * rows]
        stream = (start.astype(F32) + attended).astype(BF16)
        widened = stream.astype(F32)
        squares = jnp.sum(widened * widened, axis=1)
        scaled = (widened * gain).astype(BF16)
        if chained:
            total = chain.total(squares)

            def kv_term(t):
                weight = lax.dynamic_index_in_dim(slab_weight, t, 0, keepdims=False)
                return jnp.dot(scaled, weight, preferred_element_type=F32)

            projected = chain.reduce_scatter(kv_term)
        else:
            total = lax.psum(squares, "tensor")
            everything = lax.all_gather(scaled, "tensor", axis=1, tiled=True)
            projected = jnp.dot(everything, kv_weight, preferred_element_type=F32)
        inverse = lax.rsqrt(total / D + 1e-05)
        streams.append(stream)
        projections.append((projected * inverse[:, None]).astype(BF16))
    return jnp.concatenate(streams, axis=0), jnp.concatenate(projections, axis=0)


def solution(mesh):
    return jax.shard_map(
        on_device,
        mesh=mesh,
        in_specs=(
            P(("groups", "seq"), "tensor"),
            P(("groups", "seq"), None),
            P(("groups", "seq"), None),
            P(("groups", "seq"), "tensor"),
            P("tensor", None),
            P("tensor"),
            P(None, "tensor"),
        ),
        out_specs=(P(("groups", "seq"), "tensor"), P(("groups", "seq"), "tensor")),
        check_vma=False,
    )
```

```python
import functools
import math

import jax
import jax.numpy as jnp
from jax import lax
from jax.experimental import pallas as pl
from jax.experimental.pallas import tpu as pltpu
from jax.sharding import PartitionSpec as P

D = 16384
Q_HEADS = 128
KV_HEADS = 8
HEAD = 128
ATTEND_PARTS = 2
F32 = jnp.float32
BF16 = jnp.bfloat16
LOGIT = HEAD ** (-0.5) * math.log2(math.e)


def attend_kernel(parts, seq_ref, q_ref, ek_ref, ev_ref, k_ref, v_ref, out_ref):
    rows = q_ref.shape[0] // parts
    contract = (((1,), (1,)), ((), ()))
    shape = (rows, rows)
    hidden = lax.broadcasted_iota(jnp.int32, shape, 1) > lax.broadcasted_iota(
        jnp.int32, shape, 0
    )
    for part in range(parts):
        here = pl.ds(part * rows, rows)
        q = q_ref[here]
        early = lax.dot_general(q, ek_ref[...], contract, preferred_element_type=F32)
        early = jnp.where(seq_ref[0] > 0, early, -1e30)
        edge = lax.dot_general(q, k_ref[here], contract, preferred_element_type=F32)
        edge = jnp.where(hidden, -1e30, edge)
        pieces = [(early, ev_ref[...]), (edge, v_ref[here])]
        if part:
            before = pl.ds(0, part * rows)
            own = lax.dot_general(q, k_ref[before], contract, preferred_element_type=F32)
            pieces.append((own, v_ref[before]))
        peak = functools.reduce(
            jnp.maximum, [jnp.max(p, axis=1, keepdims=True) for p, _ in pieces]
        )
        total, context = 0.0, 0.0
        for scores, value in pieces:
            weights = jnp.exp2((scores - peak) * LOGIT)
            total += jnp.sum(weights, axis=1, keepdims=True)
            context += jnp.dot(weights.astype(BF16), value, preferred_element_type=F32)
        out_ref[here] = (context / total).astype(BF16)


def attend(queries, early_keys, early_values, own_keys, own_values, seq_index):
    rows = queries.shape[0]
    heads = queries.shape[1] // HEAD
    whole = pl.BlockSpec((rows, HEAD), lambda h, s: (0, 0))
    return pl.pallas_call(
        functools.partial(attend_kernel, ATTEND_PARTS),
        grid_spec=pltpu.PrefetchScalarGridSpec(
            num_scalar_prefetch=1,
            grid=(heads,),
            in_specs=[pl.BlockSpec((rows, HEAD), lambda h, s: (0, h))] + [whole] * 4,
            out_specs=pl.BlockSpec((rows, HEAD), lambda h, s: (0, h)),
        ),
        out_shape=jax.ShapeDtypeStruct((rows, heads * HEAD), BF16),
        compiler_params=pltpu.CompilerParams(vmem_limit_bytes=32 * 2**20),
        cost_estimate=pl.CostEstimate(flops=1000, bytes_accessed=1000, transcendentals=0),
    )(seq_index, queries, early_keys, early_values, own_keys, own_values)


def slab_kernel(at_ref, left_ref, right_ref, out_ref):
    out_ref[...] = jnp.dot(
        left_ref[...], right_ref[...], preferred_element_type=F32
    ).astype(out_ref.dtype)


def slab_dot(left, weight, at, width, dtype):
    rows, depth = left.shape
    tile = min(width, 512)
    tiles = width // tile
    return pl.pallas_call(
        slab_kernel,
        grid_spec=pltpu.PrefetchScalarGridSpec(
            num_scalar_prefetch=1,
            grid=(tiles,),
            in_specs=[
                pl.BlockSpec((rows, depth), lambda i, at: (0, 0)),
                pl.BlockSpec((depth, tile), lambda i, at: (0, at[0] * tiles + i)),
            ],
            out_specs=pl.BlockSpec((rows, tile), lambda i, at: (0, i)),
        ),
        out_shape=jax.ShapeDtypeStruct((rows, width), dtype),
        compiler_params=pltpu.CompilerParams(vmem_limit_bytes=32 * 2**20),
        cost_estimate=pl.CostEstimate(flops=1000, bytes_accessed=1000, transcendentals=0),
    )(jnp.reshape(at, (1,)), left, weight)


def together(*values):
    return lax.optimization_barrier(values)


def over(block, pairs):
    return lax.ppermute(block, "tensor", pairs)


def by_xor(block, step):
    return over(block, [(i, i ^ step) for i in range(8)])


def to_middle(block):
    return over(block, [(0, 2), (1, 3), (6, 4), (7, 5)])


def across(block):
    return over(block, [(2, 4), (3, 5), (4, 2), (5, 3)])


def place():
    t = lax.axis_index("tensor")
    z, y = t // 2, t % 2
    low = z < 2
    far = jnp.where(low, 3, 0)
    near = jnp.where(low, 2, 1)
    return z, y, (far, near, 6 - far - near - z, z)


def weight_over_y(weight):
    z, y, _ = place()
    depth, columns = weight.shape
    part = depth // 32
    quarter = lax.axis_index("groups") * 2 + lax.axis_index("seq")
    blocks = weight.reshape(4, 2, 4, part, columns)
    blocks = lax.dynamic_index_in_dim(blocks, quarter, 2, keepdims=False)
    kept = lax.dynamic_index_in_dim(blocks, y, 1, keepdims=False)
    sent = lax.dynamic_index_in_dim(blocks, 1 - y, 1, keepdims=False)
    return kept, by_xor(sent, 1)


def weight_over_z(kept, got):
    z, y, _ = place()
    first = y == 0
    pair = jnp.stack([jnp.where(first, kept, got), jnp.where(first, got, kept)], axis=1)
    pieces = []
    for step in range(4):
        piece = lax.dynamic_index_in_dim(pair, z ^ step, 0, keepdims=True)
        pieces.append(by_xor(piece, 2 * step) if step else piece)
    return pieces


def weight_in_order(pieces):
    z, _, _ = place()
    mine = jnp.zeros((4,) + pieces[0].shape[1:], pieces[0].dtype)
    for step, piece in enumerate(pieces):
        mine = lax.dynamic_update_slice_in_dim(mine, piece, z ^ step, 0)
    return mine.reshape((8,) + mine.shape[2:])


SWAP = [(0, 1), (1, 0)]


def weight_over_seq(mine, other):
    group, seq = lax.axis_index("groups"), lax.axis_index("seq")
    part = mine.shape[1]
    whole = jnp.zeros((8, 4 * part, mine.shape[2]), mine.dtype)
    beside = lax.ppermute((mine, other), "seq", SWAP)
    for block, g, s in (
        (mine, group, seq),
        (other, 1 - group, seq),
        (beside[0], group, 1 - seq),
        (beside[1], 1 - group, 1 - seq),
    ):
        whole = lax.dynamic_update_slice_in_dim(whole, block, (g * 2 + s) * part, 1)
    return whole


def kv_sum(scaled, weight):
    z, y, _ = place()
    high, low = z // 2, z % 2
    rows, depth = scaled.shape
    columns = weight.shape[2]
    blocks = weight.reshape(2, 2, 2, depth, columns)

    def terms(half):
        block = lax.dynamic_index_in_dim(blocks, half, 2, keepdims=False)
        return jnp.einsum("rk,hlkc->hlrc", scaled, block, preferred_element_type=F32)

    got = by_xor(terms(1 - y).astype(BF16), 1)
    block = terms(y) + got.astype(F32)
    for half, step in ((high, 4), (low, 2)):
        leaving = lax.dynamic_index_in_dim(block, 1 - half, 0, keepdims=False)
        staying = lax.dynamic_index_in_dim(block, half, 0, keepdims=False)
        block = staying + by_xor(leaving.astype(BF16), step).astype(F32)
    return block


def row_total(squares):
    for step in (1, 4, 2):
        squares = squares + by_xor(squares, step)
    return squares


def chained(residual, out_weight, gain, kv_weight, attend_all):
    z, y, order = place()
    width = residual.shape[1]
    wide = lambda block: block.astype(F32)
    kept, got = weight_over_y(kv_weight)
    context = attend_all()

    def sent_term(j):
        return slab_dot(context, out_weight, 2 * order[j] + 1 - y, width, BF16)

    def own_term(j):
        return slab_dot(context, out_weight, 2 * order[j] + y, width, F32)

    context, kept, got = together(context, kept, got)
    relay = weight_over_z(kept, got)
    leaving = sent_term(0)
    leaving, context = together(leaving, context)
    y_got = by_xor(leaving, 1)
    term, leaving = own_term(0), sent_term(1)
    y_got, term, leaving, context, *relay = together(y_got, term, leaving, context, *relay)
    relay = weight_in_order(relay)
    far = term + wide(y_got)
    y_got = by_xor(leaving, 1)
    far_got = to_middle(far.astype(BF16))
    term, leaving = own_term(1), sent_term(2)
    y_got, far_got, term, leaving, context, relay = together(
        y_got, far_got, term, leaving, context, relay
    )
    near = term + wide(y_got)
    y_got = by_xor(leaving, 1)
    far_got = across((far + wide(far_got)).astype(BF16))
    near_got = to_middle(near.astype(BF16))
    other = lax.ppermute(relay, "groups", SWAP)
    term, leaving, own = own_term(2), sent_term(3), own_term(3)
    y_got, far_got, near_got, term, leaving, own = together(
        y_got, far_got, near_got, term, leaving, own
    )
    last = term + wide(y_got) + wide(far_got)
    y_got = by_xor(leaving, 1)
    last_got = by_xor(last.astype(BF16), 2)
    near_got = across((near + wide(near_got)).astype(BF16))
    slab_weight = weight_over_seq(relay, other)
    y_got, last_got, near_got, own, slab_weight = together(
        y_got, last_got, near_got, own, slab_weight
    )
    attended = own + wide(y_got) + wide(near_got) + wide(last_got)
    stream = (wide(residual) + attended).astype(BF16)
    widened = wide(stream)
    total = row_total(jnp.sum(widened * widened, axis=1))
    inverse = lax.rsqrt(total / D + 1e-05)
    projected = kv_sum((widened * gain).astype(BF16), slab_weight)
    return stream, (projected * inverse[:, None]).astype(BF16)


def gathered(residual, out_weight, gain, kv_weight, attend_all):
    partial = jnp.dot(attend_all(), out_weight, preferred_element_type=F32)
    attended = lax.psum_scatter(
        partial.astype(BF16), "tensor", scatter_dimension=1, tiled=True
    ).astype(F32)
    stream = (residual.astype(F32) + attended).astype(BF16)
    widened = stream.astype(F32)
    total = lax.psum(jnp.sum(widened * widened, axis=1), "tensor")
    inverse = lax.rsqrt(total / D + 1e-05)
    scaled = (widened * gain).astype(BF16)
    everything = lax.all_gather(scaled, "tensor", axis=1, tiled=True)
    projected = jnp.dot(everything, kv_weight, preferred_element_type=F32)
    return stream, (projected * inverse[:, None]).astype(BF16)


def on_device(queries, keys, values, residual, out_weight, norm_gain, kv_weight):
    heads_here = queries.shape[1] // HEAD
    devices = lax.axis_size("tensor")
    tensor_rank = lax.axis_index("tensor")
    seq_index = lax.axis_index("seq")
    kv_group = tensor_rank * heads_here // (Q_HEADS // KV_HEADS)
    own_keys = lax.dynamic_slice_in_dim(keys, kv_group * HEAD, HEAD, 1)
    own_values = lax.dynamic_slice_in_dim(values, kv_group * HEAD, HEAD, 1)
    early_keys, early_values = lax.ppermute((own_keys, own_values), "seq", [(0, 1)])
    gain = norm_gain.astype(F32)[None, :]

    def attend_all():
        return attend(
            queries, early_keys, early_values, own_keys, own_values, seq_index.reshape(1)
        )

    summed = chained if devices == 8 else gathered
    return summed(residual, out_weight, gain, kv_weight, attend_all)


def solution(mesh):
    return jax.shard_map(
        on_device,
        mesh=mesh,
        in_specs=(
            P(("groups", "seq"), "tensor"),
            P(("groups", "seq"), None),
            P(("groups", "seq"), None),
            P(("groups", "seq"), "tensor"),
            P("tensor", None),
            P("tensor"),
            P(None, "tensor"),
        ),
        out_specs=(P(("groups", "seq"), "tensor"), P(("groups", "seq"), "tensor")),
        check_vma=False,
    )
```

```python
import functools
import math

import jax
import jax.numpy as jnp
from jax import lax
from jax.experimental import pallas as pl
from jax.experimental.pallas import tpu as pltpu
from jax.sharding import PartitionSpec as P

D = 16384
Q_HEADS = 128
KV_HEADS = 8
HEAD = 128
F32 = jnp.float32
BF16 = jnp.bfloat16
LOGIT = HEAD ** (-0.5) * math.log2(math.e)
SWAP = [(0, 1), (1, 0)]
EXTRA = 16
PARAMS = pltpu.CompilerParams(vmem_limit_bytes=40 * 2**20)
BRIEF = pl.CostEstimate(flops=1000, bytes_accessed=1000, transcendentals=0)


def wide(block):
    return block.astype(F32)


def attend_kernel(seq_ref, q_ref, ek_ref, ev_ref, k_ref, v_ref, out_ref):
    contract = (((1,), (1,)), ((), ()))
    shape = (q_ref.shape[0], k_ref.shape[0])
    hidden = lax.broadcasted_iota(jnp.int32, shape, 1) > lax.broadcasted_iota(
        jnp.int32, shape, 0
    )

    def heads(with_earlier):
        for head in range(q_ref.shape[1] // HEAD):
            here = pl.ds(head * HEAD, HEAD)
            q = q_ref[:, here]
            scores = lambda keys: lax.dot_general(q, keys, contract, preferred_element_type=F32)
            pieces = [(jnp.where(hidden, -1e30, scores(k_ref[...])), v_ref)]
            if with_earlier:
                pieces.append((scores(ek_ref[...]), ev_ref))
            peak = functools.reduce(
                jnp.maximum, [jnp.max(p, axis=1, keepdims=True) for p, _ in pieces]
            )
            both = 0.0
            for piece, value_ref in pieces:
                weights = jnp.exp2((piece - peak) * LOGIT).astype(BF16)
                value = value_ref[...]
                beside = jnp.concatenate([value, jnp.ones_like(value)], axis=1)
                both += jnp.dot(weights, beside, preferred_element_type=F32)
            out_ref[:, here] = (both[:, :HEAD] / both[:, HEAD:]).astype(BF16)

    pl.when(seq_ref[0] > 0)(lambda: heads(True))
    pl.when(seq_ref[0] == 0)(lambda: heads(False))


def attend(seq_index, queries, earlier, own):
    rows, columns = queries.shape
    some = min(8, columns // HEAD) * HEAD
    block = pl.BlockSpec((rows, some), lambda h, s: (0, h))
    head = lambda i: pl.BlockSpec((rows, HEAD), lambda h, s: (0, i))
    return pl.pallas_call(
        attend_kernel,
        grid_spec=pltpu.PrefetchScalarGridSpec(
            num_scalar_prefetch=1,
            grid=(columns // some,),
            in_specs=[block, head(0), head(1), head(0), head(1)],
            out_specs=block,
        ),
        out_shape=jax.ShapeDtypeStruct((rows, columns), BF16),
        compiler_params=PARAMS,
        cost_estimate=BRIEF,
    )(seq_index, queries, earlier, earlier, own, own)


def slab_kernel(cuts, at_ref, left_ref, right_ref, *out_refs):
    product = jnp.dot(left_ref[...], right_ref[...], preferred_element_type=F32)
    first = 0
    for rows, out_ref in zip(cuts, out_refs, strict=True):
        out_ref[...] = product[first : first + rows].astype(out_ref.dtype)
        first += rows


def slab_dot(left, weight, at, width, dtype, span=None, cuts=None):
    depth = left.shape[1]
    first, last = span or (0, left.shape[0])
    rows = last - first
    cuts = cuts or (rows,)
    tile = min(width, 1024)
    tiles = width // tile
    return pl.pallas_call(
        functools.partial(slab_kernel, cuts),
        grid_spec=pltpu.PrefetchScalarGridSpec(
            num_scalar_prefetch=1,
            grid=(tiles,),
            in_specs=[
                pl.BlockSpec((rows, depth), lambda i, at: (first // rows, 0)),
                pl.BlockSpec((depth, tile), lambda i, at: (0, at[0] * tiles + i)),
            ],
            out_specs=[pl.BlockSpec((n, tile), lambda i, at: (0, i)) for n in cuts],
        ),
        out_shape=[jax.ShapeDtypeStruct((n, width), dtype) for n in cuts],
        compiler_params=PARAMS,
        cost_estimate=BRIEF,
    )(jnp.reshape(at, (1,)), left, weight)


def put_squares(out_ref, squares):
    rows = out_ref.shape[0] - EXTRA
    high = squares.astype(BF16)
    low = (squares - wide(high)).astype(BF16)
    line = lax.broadcasted_iota(jnp.int32, (EXTRA, squares.shape[1]), 0)
    both = jnp.where(line == 0, wide(high), jnp.where(line == 1, wide(low), 0.0))
    out_ref[rows:] = both.astype(BF16)


def kv_kernel(at_ref, *refs):
    lefts, rights, rest = refs[:4], refs[4:8], refs[8:]
    out_ref = rest[-1]
    rows = lefts[0].shape[0]
    for i in range(out_ref.shape[0]):
        total = 0.0
        for left, right in zip(lefts, rights, strict=True):
            total += jnp.dot(left[...], right[0, i], preferred_element_type=F32)
        out_ref[i, :rows] = total.astype(out_ref.dtype)
        if len(rest) == 2:
            put_squares(out_ref.at[i], rest[0][...])


def kv_dot(scaled, quarters, parts, side, squares=None):
    rows = scaled.shape[0]
    _, _, part, columns = parts[0].shape
    step = 2
    left = lambda q: pl.BlockSpec((rows, part), lambda i, at: (0, at[q]))
    right = pl.BlockSpec((1, step, part, columns), lambda i, at: (side, i, 0, 0))
    beside = [] if squares is None else [squares]
    total, dtype = (rows, F32) if squares is None else (rows + EXTRA, BF16)
    return pl.pallas_call(
        kv_kernel,
        grid_spec=pltpu.PrefetchScalarGridSpec(
            num_scalar_prefetch=1,
            grid=(4 // step,),
            in_specs=[left(q) for q in range(4)]
            + [right] * 4
            + [pl.BlockSpec((1, columns), lambda i, at: (0, 0))] * len(beside),
            out_specs=pl.BlockSpec((step, total, columns), lambda i, at: (i, 0, 0)),
        ),
        out_shape=jax.ShapeDtypeStruct((4, total, columns), dtype),
        compiler_params=PARAMS,
        cost_estimate=BRIEF,
    )(quarters, *[scaled] * 4, *parts, *beside)


def kv_pair_kernel(kept_ref, got_ref, squares_ref, own_ref, total_ref, *sent_refs):
    rows = kept_ref.shape[1]
    given = wide(got_ref[0, rows:])
    squares = squares_ref[...] + given[0:1] + given[1:2]
    total_ref[...] = squares
    own_ref[...] = kept_ref[0] + wide(got_ref[0, :rows])
    for i, sent_ref in enumerate(sent_refs, 1):
        sent_ref[:rows] = (kept_ref[i] + wide(got_ref[i, :rows])).astype(BF16)
        put_squares(sent_ref, squares)


def kv_sum(kept, got, squares):
    rows, columns = kept.shape[1:]
    own, total, *sent = pl.pallas_call(
        kv_pair_kernel,
        out_shape=[
            jax.ShapeDtypeStruct((rows, columns), F32),
            jax.ShapeDtypeStruct((1, columns), F32),
        ]
        + [jax.ShapeDtypeStruct((rows + EXTRA, columns), BF16)] * 3,
        compiler_params=PARAMS,
        cost_estimate=BRIEF,
    )(kept, got, squares)
    return own, total, [by_xor(sent[i - 1], 2 * i) for i in (3, 2, 1)]


def kv_finish(own, total, arrived):
    rows = own.shape[0]
    for block in arrived:
        own = own + wide(block[:rows])
        total = total + wide(block[rows : rows + 1]) + wide(block[rows + 1 : rows + 2])
    inverse = lax.rsqrt(total[0, :rows] / D + 1e-05)
    return (own * inverse[:, None]).astype(BF16)


def together(*values):
    return lax.optimization_barrier(values)


def over(block, pairs):
    return lax.ppermute(block, "tensor", pairs)


def by_xor(block, step):
    return over(block, [(i, i ^ step) for i in range(8)])


def to_middle(block):
    return over(block, [(0, 2), (1, 3), (6, 4), (7, 5)])


def across(block):
    return over(block, [(2, 4), (3, 5), (4, 2), (5, 3)])


def place():
    t = lax.axis_index("tensor")
    z, y = t // 2, t % 2
    low = z < 2
    far = jnp.where(low, 3, 0)
    near = jnp.where(low, 2, 1)
    return z, y, (far, near, 6 - far - near - z, z)


def weight_blocks(weight, quarter, side):
    depth, columns = weight.shape
    blocks = weight.reshape(4, 2, 4, depth // 32, columns)
    blocks = lax.dynamic_index_in_dim(blocks, side, 1, keepdims=False)
    return lax.dynamic_index_in_dim(blocks, quarter, 1, keepdims=False)


def weight_over_z(blocks, steps):
    z = place()[0]
    pieces = [lax.dynamic_index_in_dim(blocks, z ^ i, 0, keepdims=False) for i in steps]
    return [by_xor(piece, 2 * i) if i else piece for i, piece in zip(steps, pieces)]


def chained(attend_all, residual, out_weight, gain, kv_weight):
    z, y, order = place()
    tokens, width = residual.shape
    columns = kv_weight.shape[1]
    quarter = lax.axis_index("groups") * 2 + lax.axis_index("seq")
    quarters = jnp.stack([quarter, quarter ^ 2, quarter ^ 1, quarter ^ 3])
    half = tokens // 2
    cuts = (half, half)

    def sent_term(j):
        return slab_dot(context, out_weight, 2 * order[j] + 1 - y, width, BF16, cuts=cuts)

    def own_term(j):
        return slab_dot(context, out_weight, 2 * order[j] + y, width, F32, cuts=cuts)

    got = by_xor(weight_blocks(kv_weight, quarter, 1 - y), 1)
    context = attend_all()
    kept = weight_blocks(kv_weight, quarter, y)
    pieces = weight_over_z(kept, (0, 1, 2, 3))
    *leaving, context, got, p1, p2, p3 = together(*sent_term(0), context, got, *pieces[1:])
    arriving = [by_xor(block, 1) for block in leaving]
    pieces = [pieces[0], p1, p2, p3]
    other_pieces = weight_over_z(got, (0, 1, 2, 3))
    own = own_term(0)
    arriving += [by_xor(block, 1) for block in sent_term(1)]
    started = []
    far, near, streams, sums = [], [], [], []
    for h in range(8):
        j, side = divmod(h, 2)
        moved = started[h - 2] if h > 1 else other_pieces[1:] if h == 0 else []
        here, context, *rest = together(arriving[h], context, *own, *moved)
        own, moved = rest[:2], rest[2:]
        term = own[side] + wide(here)
        if j == 0:
            far.append(term)
            started.append([to_middle(term.astype(BF16))])
        if j == 1:
            near.append(term)
            far_sent = (far[side] + wide(moved[0])).astype(BF16)
            started.append([across(far_sent), to_middle(term.astype(BF16))])
        if j == 2:
            last_sent = (term + wide(moved[0])).astype(BF16)
            near_sent = (near[side] + wide(moved[1])).astype(BF16)
            started.append([by_xor(last_sent, 2), across(near_sent)])
        if j == 3:
            attended = term + wide(moved[0]) + wide(moved[1])
            first = side * half
            stream = (wide(residual[first : first + half]) + attended).astype(BF16)
            widened = wide(stream)
            squares = jnp.sum(widened * widened, axis=1)
            squares = jnp.pad(squares, (0, columns - half)).reshape(1, columns)
            scaled = (widened * gain).astype(BF16)
            streams.append(stream)
            leaving = kv_dot(scaled, quarters, parts, 1, squares)
            staying = kv_dot(scaled, quarters, parts, 0)
            sums.append((staying, by_xor(leaving, 1), squares))
        if h == 0:
            mine = jnp.stack([*pieces, other_pieces[0], *moved]).reshape((2, *kept.shape))
            other = lax.ppermute(mine, "groups", SWAP)
        if h == 4:
            mine, other, context = together(mine, other, context)
            parts = [mine, other] + [lax.ppermute(p, "seq", SWAP) for p in (mine, other)]
        if h == 5:
            *parts, context = together(*parts, context)
        if side == 0 and j < 3:
            following = own_term(j + 1)
            if j < 2:
                arriving += [by_xor(block, 1) for block in sent_term(j + 2)]
        if side == 1 and j < 3:
            own = following
    projected = [kv_finish(*kv_sum(*terms)) for terms in sums]
    return jnp.concatenate(streams, axis=0), jnp.concatenate(projected, axis=0)


def gathered(attend_all, residual, out_weight, gain, kv_weight):
    context = attend_all()
    partial = jnp.dot(context, out_weight, preferred_element_type=F32)
    attended = lax.psum_scatter(partial.astype(BF16), "tensor", scatter_dimension=1, tiled=True)
    stream = (wide(residual) + wide(attended)).astype(BF16)
    widened = wide(stream)
    total = lax.psum(jnp.sum(widened * widened, axis=1), "tensor")
    inverse = lax.rsqrt(total / D + 1e-05)
    everything = lax.all_gather((widened * gain).astype(BF16), "tensor", axis=1, tiled=True)
    projected = jnp.dot(everything, kv_weight, preferred_element_type=F32)
    return stream, (projected * inverse[:, None]).astype(BF16)


def on_device(queries, keys, values, residual, out_weight, norm_gain, kv_weight):
    heads_here = queries.shape[1] // HEAD
    devices = lax.axis_size("tensor")
    tensor_rank = lax.axis_index("tensor")
    seq_index = lax.axis_index("seq").reshape(1)
    kv_group = tensor_rank * heads_here // (Q_HEADS // KV_HEADS)
    head = lambda heads: lax.dynamic_slice_in_dim(heads, kv_group * HEAD, HEAD, 1)
    own = jnp.concatenate([head(keys), head(values)], axis=1)
    earlier = lax.ppermute(own, "seq", [(0, 1)])
    attend_all = functools.partial(attend, seq_index, queries, earlier, own)
    summed = chained if devices == 8 else gathered
    gain = wide(norm_gain)[None, :]
    return summed(attend_all, residual, out_weight, gain, kv_weight)


def solution(mesh):
    return jax.shard_map(
        on_device,
        mesh=mesh,
        in_specs=(
            P(("groups", "seq"), "tensor"),
            P(("groups", "seq"), None),
            P(("groups", "seq"), None),
            P(("groups", "seq"), "tensor"),
            P("tensor", None),
            P("tensor"),
            P(None, "tensor"),
        ),
        out_specs=(P(("groups", "seq"), "tensor"), P(("groups", "seq"), "tensor")),
        check_vma=False,
    )
```

```python
import functools
import math

import jax
import jax.numpy as jnp
from jax import lax
from jax.experimental import pallas as pl
from jax.experimental.pallas import tpu as pltpu
from jax.sharding import PartitionSpec as P

D = 16384
Q_HEADS = 128
KV_HEADS = 8
HEAD = 128
F32 = jnp.float32
BF16 = jnp.bfloat16
LOGIT = HEAD ** (-0.5) * math.log2(math.e)
SWAP = [(0, 1), (1, 0)]
EXTRA = 16
PARAMS = pltpu.CompilerParams(vmem_limit_bytes=40 * 2**20)
BRIEF = pl.CostEstimate(flops=1000, bytes_accessed=1000, transcendentals=0)


def wide(block):
    return block.astype(F32)


def attend_kernel(seq_ref, q_ref, ek_ref, ev_ref, k_ref, v_ref, out_ref):
    contract = (((1,), (1,)), ((), ()))
    shape = (q_ref.shape[0], k_ref.shape[0])
    hidden = lax.broadcasted_iota(jnp.int32, shape, 1) > lax.broadcasted_iota(
        jnp.int32, shape, 0
    )

    def heads(with_earlier):
        for head in range(q_ref.shape[1] // HEAD):
            here = pl.ds(head * HEAD, HEAD)
            q = q_ref[:, here]
            scores = lambda keys: lax.dot_general(q, keys, contract, preferred_element_type=F32)
            pieces = [(jnp.where(hidden, -1e30, scores(k_ref[...])), v_ref)]
            if with_earlier:
                pieces.append((scores(ek_ref[...]), ev_ref))
            peak = functools.reduce(
                jnp.maximum, [jnp.max(p, axis=1, keepdims=True) for p, _ in pieces]
            )
            both = 0.0
            for piece, value_ref in pieces:
                weights = jnp.exp2((piece - peak) * LOGIT).astype(BF16)
                value = value_ref[...]
                beside = jnp.concatenate([value, jnp.ones_like(value)], axis=1)
                both += jnp.dot(weights, beside, preferred_element_type=F32)
            out_ref[:, here] = (both[:, :HEAD] / both[:, HEAD:]).astype(BF16)

    pl.when(seq_ref[0] > 0)(lambda: heads(True))
    pl.when(seq_ref[0] == 0)(lambda: heads(False))


def attend(seq_index, queries, earlier, own):
    rows, columns = queries.shape
    some = min(8, columns // HEAD) * HEAD
    block = pl.BlockSpec((rows, some), lambda h, s: (0, h))
    head = lambda i: pl.BlockSpec((rows, HEAD), lambda h, s: (0, i))
    return pl.pallas_call(
        attend_kernel,
        grid_spec=pltpu.PrefetchScalarGridSpec(
            num_scalar_prefetch=1,
            grid=(columns // some,),
            in_specs=[block, head(0), head(1), head(0), head(1)],
            out_specs=block,
        ),
        out_shape=jax.ShapeDtypeStruct((rows, columns), BF16),
        compiler_params=PARAMS,
        cost_estimate=BRIEF,
    )(seq_index, queries, earlier, earlier, own, own)


def slab_kernel(cuts, at_ref, left_ref, right_ref, *out_refs):
    product = jnp.dot(left_ref[...], right_ref[...], preferred_element_type=F32)
    first = 0
    for rows, out_ref in zip(cuts, out_refs, strict=True):
        out_ref[...] = product[first : first + rows].astype(out_ref.dtype)
        first += rows


def slab_dot(left, weight, at, width, dtype, span=None, cuts=None):
    depth = left.shape[1]
    first, last = span or (0, left.shape[0])
    rows = last - first
    cuts = cuts or (rows,)
    tile = min(width, 1024)
    tiles = width // tile
    return pl.pallas_call(
        functools.partial(slab_kernel, cuts),
        grid_spec=pltpu.PrefetchScalarGridSpec(
            num_scalar_prefetch=1,
            grid=(tiles,),
            in_specs=[
                pl.BlockSpec((rows, depth), lambda i, at: (first // rows, 0)),
                pl.BlockSpec((depth, tile), lambda i, at: (0, at[0] * tiles + i)),
            ],
            out_specs=[pl.BlockSpec((n, tile), lambda i, at: (0, i)) for n in cuts],
        ),
        out_shape=[jax.ShapeDtypeStruct((n, width), dtype) for n in cuts],
        compiler_params=PARAMS,
        cost_estimate=pl.CostEstimate(flops=1000000000, bytes_accessed=1000, transcendentals=0),
    )(jnp.reshape(at, (1,)), left, weight)


def put_squares(out_ref, squares):
    rows = out_ref.shape[0] - EXTRA
    high = squares.astype(BF16)
    low = (squares - wide(high)).astype(BF16)
    line = lax.broadcasted_iota(jnp.int32, (EXTRA, squares.shape[1]), 0)
    both = jnp.where(line == 0, wide(high), jnp.where(line == 1, wide(low), 0.0))
    out_ref[rows:] = both.astype(BF16)


def kv_kernel(at_ref, *refs):
    lefts, rights, rest = refs[:4], refs[4:8], refs[8:]
    out_ref = rest[-1]
    rows = lefts[0].shape[0]
    for i in range(out_ref.shape[0]):
        total = 0.0
        for left, right in zip(lefts, rights, strict=True):
            total += jnp.dot(left[...], right[0, i], preferred_element_type=F32)
        out_ref[i, :rows] = total.astype(out_ref.dtype)
        if len(rest) == 2:
            put_squares(out_ref.at[i], rest[0][...])


def kv_dot(scaled, quarters, parts, side, squares=None):
    rows = scaled.shape[0]
    _, _, part, columns = parts[0].shape
    step = 2
    left = lambda q: pl.BlockSpec((rows, part), lambda i, at: (0, at[q]))
    right = pl.BlockSpec((1, step, part, columns), lambda i, at: (side, i, 0, 0))
    beside = [] if squares is None else [squares]
    total, dtype = (rows, F32) if squares is None else (rows + EXTRA, BF16)
    return pl.pallas_call(
        kv_kernel,
        grid_spec=pltpu.PrefetchScalarGridSpec(
            num_scalar_prefetch=1,
            grid=(4 // step,),
            in_specs=[left(q) for q in range(4)]
            + [right] * 4
            + [pl.BlockSpec((1, columns), lambda i, at: (0, 0))] * len(beside),
            out_specs=pl.BlockSpec((step, total, columns), lambda i, at: (i, 0, 0)),
        ),
        out_shape=jax.ShapeDtypeStruct((4, total, columns), dtype),
        compiler_params=PARAMS,
        cost_estimate=BRIEF,
    )(quarters, *[scaled] * 4, *parts, *beside)


def kv_pair_kernel(kept_ref, got_ref, squares_ref, own_ref, total_ref, *sent_refs):
    rows = kept_ref.shape[1]
    given = wide(got_ref[0, rows:])
    squares = squares_ref[...] + given[0:1] + given[1:2]
    total_ref[...] = squares
    own_ref[...] = kept_ref[0] + wide(got_ref[0, :rows])
    for i, sent_ref in enumerate(sent_refs, 1):
        sent_ref[:rows] = (kept_ref[i] + wide(got_ref[i, :rows])).astype(BF16)
        put_squares(sent_ref, squares)


def kv_sum(kept, got, squares):
    rows, columns = kept.shape[1:]
    own, total, *sent = pl.pallas_call(
        kv_pair_kernel,
        out_shape=[
            jax.ShapeDtypeStruct((rows, columns), F32),
            jax.ShapeDtypeStruct((1, columns), F32),
        ]
        + [jax.ShapeDtypeStruct((rows + EXTRA, columns), BF16)] * 3,
        compiler_params=PARAMS,
        cost_estimate=BRIEF,
    )(kept, got, squares)
    return own, total, [by_xor(sent[i - 1], 2 * i) for i in (3, 2, 1)]


def kv_finish(own, total, arrived):
    rows = own.shape[0]
    for block in arrived:
        own = own + wide(block[:rows])
        total = total + wide(block[rows : rows + 1]) + wide(block[rows + 1 : rows + 2])
    inverse = lax.rsqrt(total[0, :rows] / D + 1e-05)
    return (own * inverse[:, None]).astype(BF16)


def together(*values):
    return lax.optimization_barrier(values)


def over(block, pairs):
    return lax.ppermute(block, "tensor", pairs)


def by_xor(block, step):
    return over(block, [(i, i ^ step) for i in range(8)])


def to_middle(block):
    return over(block, [(0, 2), (1, 3), (6, 4), (7, 5)])


def across(block):
    return over(block, [(2, 4), (3, 5), (4, 2), (5, 3)])


def place():
    t = lax.axis_index("tensor")
    z, y = t // 2, t % 2
    low = z < 2
    far = jnp.where(low, 3, 0)
    near = jnp.where(low, 2, 1)
    return z, y, (far, near, 6 - far - near - z, z)


def weight_blocks(weight, quarter, side):
    depth, columns = weight.shape
    blocks = weight.reshape(4, 2, 4, depth // 32, columns)
    blocks = lax.dynamic_index_in_dim(blocks, side, 1, keepdims=False)
    return lax.dynamic_index_in_dim(blocks, quarter, 1, keepdims=False)


def weight_over_z(blocks, steps):
    z = place()[0]
    pieces = [lax.dynamic_index_in_dim(blocks, z ^ i, 0, keepdims=False) for i in steps]
    return [by_xor(piece, 2 * i) if i else piece for i, piece in zip(steps, pieces)]


def chained(attend_all, residual, out_weight, gain, kv_weight):
    z, y, order = place()
    tokens, width = residual.shape
    columns = kv_weight.shape[1]
    quarter = lax.axis_index("groups") * 2 + lax.axis_index("seq")
    quarters = jnp.stack([quarter, quarter ^ 2, quarter ^ 1, quarter ^ 3])
    half = tokens // 2
    cuts = (half, half)

    def sent_term(j):
        return slab_dot(context, out_weight, 2 * order[j] + 1 - y, width, BF16, cuts=cuts)

    def own_term(j):
        return slab_dot(context, out_weight, 2 * order[j] + y, width, F32, cuts=cuts)

    got = by_xor(weight_blocks(kv_weight, quarter, 1 - y), 1)
    context = attend_all()
    kept = weight_blocks(kv_weight, quarter, y)
    pieces = weight_over_z(kept, (0, 1, 2, 3))
    *leaving, context, got, p1, p2, p3 = together(*sent_term(0), context, got, *pieces[1:])
    arriving = [by_xor(block, 1) for block in leaving]
    pieces = [pieces[0], p1, p2, p3]
    other_pieces = weight_over_z(got, (0, 1, 2, 3))
    own = own_term(0)
    arriving += [by_xor(block, 1) for block in sent_term(1)]
    started = []
    far, near, streams, sums = [], [], [], []
    for h in range(8):
        j, side = divmod(h, 2)
        moved = started[h - 2] if h > 1 else other_pieces[1:] if h == 0 else []
        values = [arriving[h], context, *own, *moved]
        if h == 7:
            values += sums[0][:2]
        here, context, *rest = together(*values)
        own, moved = rest[:2], rest[2:]
        if h == 7:
            sums[0][0], sums[0][1] = moved[2:]
        term = own[side] + wide(here)
        if j == 0:
            far.append(term)
            started.append([to_middle(term.astype(BF16))])
        if j == 1:
            near.append(term)
            far_sent = (far[side] + wide(moved[0])).astype(BF16)
            started.append([across(far_sent), to_middle(term.astype(BF16))])
        if j == 2:
            last_sent = (term + wide(moved[0])).astype(BF16)
            near_sent = (near[side] + wide(moved[1])).astype(BF16)
            started.append([by_xor(last_sent, 2), across(near_sent)])
        if j == 3:
            attended = term + wide(moved[0]) + wide(moved[1])
            first = side * half
            stream = (wide(residual[first : first + half]) + attended).astype(BF16)
            widened = wide(stream)
            squares = jnp.sum(widened * widened, axis=1)
            squares = jnp.pad(squares, (0, columns - half)).reshape(1, columns)
            scaled = (widened * gain).astype(BF16)
            streams.append(stream)
            leaving = kv_dot(scaled, quarters, parts, 1, squares)
            staying = kv_dot(scaled, quarters, parts, 0)
            sums.append([staying, leaving, squares])
        if h == 0:
            mine = jnp.stack([*pieces, other_pieces[0], *moved]).reshape((2, *kept.shape))
            other = lax.ppermute(mine, "groups", SWAP)
        if h == 4:
            mine, other, context = together(mine, other, context)
            parts = [mine, other] + [lax.ppermute(p, "seq", SWAP) for p in (mine, other)]
        if h == 5:
            *parts, context = together(*parts, context)
        if side == 0 and j < 3:
            following = own_term(j + 1)
            if j < 2:
                arriving += [by_xor(block, 1) for block in sent_term(j + 2)]
        if side == 1 and j < 3:
            own = following
    sums = [(staying, by_xor(leaving, 1), squares) for staying, leaving, squares in sums]
    projected = [kv_finish(*kv_sum(*terms)) for terms in sums]
    return jnp.concatenate(streams, axis=0), jnp.concatenate(projected, axis=0)


def gathered(attend_all, residual, out_weight, gain, kv_weight):
    context = attend_all()
    partial = jnp.dot(context, out_weight, preferred_element_type=F32)
    attended = lax.psum_scatter(partial.astype(BF16), "tensor", scatter_dimension=1, tiled=True)
    stream = (wide(residual) + wide(attended)).astype(BF16)
    widened = wide(stream)
    total = lax.psum(jnp.sum(widened * widened, axis=1), "tensor")
    inverse = lax.rsqrt(total / D + 1e-05)
    everything = lax.all_gather((widened * gain).astype(BF16), "tensor", axis=1, tiled=True)
    projected = jnp.dot(everything, kv_weight, preferred_element_type=F32)
    return stream, (projected * inverse[:, None]).astype(BF16)


def on_device(queries, keys, values, residual, out_weight, norm_gain, kv_weight):
    heads_here = queries.shape[1] // HEAD
    devices = lax.axis_size("tensor")
    tensor_rank = lax.axis_index("tensor")
    seq_index = lax.axis_index("seq").reshape(1)
    kv_group = tensor_rank * heads_here // (Q_HEADS // KV_HEADS)
    head = lambda heads: lax.dynamic_slice_in_dim(heads, kv_group * HEAD, HEAD, 1)
    own = jnp.concatenate([head(keys), head(values)], axis=1)
    earlier = lax.ppermute(own, "seq", [(0, 1)])
    attend_all = functools.partial(attend, seq_index, queries, earlier, own)
    summed = chained if devices == 8 else gathered
    gain = wide(norm_gain)[None, :]
    return summed(attend_all, residual, out_weight, gain, kv_weight)


def solution(mesh):
    return jax.shard_map(
        on_device,
        mesh=mesh,
        in_specs=(
            P(("groups", "seq"), "tensor"),
            P(("groups", "seq"), None),
            P(("groups", "seq"), None),
            P(("groups", "seq"), "tensor"),
            P("tensor", None),
            P("tensor"),
            P(None, "tensor"),
        ),
        out_specs=(P(("groups", "seq"), "tensor"), P(("groups", "seq"), "tensor")),
        check_vma=False,
    )
```
